128 devices in a mesh: dp: 16 (over x, z), tensor: 8 (over y, core).
Axes of the slice: x: 4, y: 4, z: 4, core: 2. Of those that a mesh axis runs over, the one named last changes fastest.
Arguments:
- activations: bfloat16 [4, 16384, 4096], P(None, 'dp', 'tensor'), may hold values from -6 to 6
- out_grads: bfloat16 [4, 16384, 14336], P(None, 'dp', 'tensor'), may hold values from -6 to 6
- proj_input: bfloat16 [4, 64, 4096], P(None, None, 'tensor'), may hold values from -0.09375 to 0.09375
- proj_output: bfloat16 [4, 64, 14336], P(None, None, 'tensor'), may hold values from -0.046875 to 0.046875
- query_feats: bfloat16 [4, 512, 4096], P(None, 'tensor', 'dp'), may hold values from -6 to 6
Outputs:
- scores: float32 [16384, 512], P('dp', 'tensor')
The draws below stay inside these ranges and needn't reach their ends.
All inputs are finite; a program needn't handle non-finite values.
Results may differ from the reference program's by a relative error of at most 0.0029.
Values may be sent and summed in bfloat16 or wider, within the bound.
No kernel may reach another device: no remote copies, remote signals or barrier semaphores. Data moves between devices by JAX's collectives and lax.ppermute only.
A program may use at most 192 MiB of HBM per device.

```python
import jax
import jax.numpy as jnp
from jax import lax

D = 4096
FF = 14336
R = 64
LAYERS = 4
Q = 512
TOKENS = 16384


def block_levels(key, dims, cuts, smallest, largest):
    factor_of, own = 1.0, jax.random.fold_in(key, 6)
    for dim, parts in cuts:
        heights = jnp.exp(jax.random.uniform(jax.random.fold_in(own, dim), (parts,), jnp.float32, smallest / len(cuts), largest / len(cuts)))
        factor_of = factor_of * jnp.repeat(heights, dims[dim] // parts).reshape([-1 if axis == dim else 1 for axis in range(len(dims))])
    return factor_of


def bell_draw(rng, shape, spread, most, shards=(), dtype=jnp.bfloat16):
    array = spread * jax.random.normal(rng, shape, jnp.float32)
    if shards:
        array = array * block_levels(rng, shape, shards, -0.22, 0.18)
    return jnp.clip(array, -most, most).astype(dtype)


def setup_inputs(seed: int = 0) -> dict:
    streams_of = jax.random.split(jax.random.key(seed), 6)
    return {
        "activations": bell_draw(streams_of[0], (LAYERS, TOKENS, D), 1.0, 6.0, ((1, 16), (2, 8))),
        "out_grads": bell_draw(streams_of[1], (LAYERS, TOKENS, FF), 1.0, 6.0, ((1, 16), (2, 8))),
        "proj_input": bell_draw(streams_of[2], (LAYERS, R, D), D ** -0.5, 0.09375, ((2, 8),)),
        "proj_output": bell_draw(streams_of[3], (LAYERS, R, FF), FF ** -0.5, 0.046875, ((2, 8),)),
        "query_feats": bell_draw(streams_of[4], (LAYERS, Q, R * R), 1.0, 6.0, ((1, 8), (2, 16))),
    }


def reference(activations, out_grads, proj_input, proj_output, query_feats):
    tokens_all = activations.shape[1]
    width = proj_input.shape[1]
    scale = (activations.shape[0] * width * width) ** -0.5

    def layer(total, items):
        acts, grads, p_in, p_out, queries = items
        in_proj = jnp.dot(acts, p_in.T, preferred_element_type=jnp.float32)
        out_proj = jnp.dot(grads, p_out.T, preferred_element_type=jnp.float32)
        features = (in_proj[:, :, None] * out_proj[:, None, :]).reshape(tokens_all, width * width).astype(jnp.bfloat16)
        return total + jnp.dot(features, queries.T, preferred_element_type=jnp.float32), None

    start = jnp.zeros((tokens_all, query_feats.shape[1]), jnp.float32)
    total, unused = lax.scan(layer, start, (activations, out_grads, proj_input, proj_output, query_feats))
    return total * scale
```

```python
import functools

import jax
import jax.numpy as jnp
from jax import lax
from jax.experimental import pallas as pl
from jax.experimental.pallas import tpu as pltpu
from jax.sharding import PartitionSpec as P

NT = (((1,), (1,)), ((), ()))
PROJECT_VMEM = 61 * 2**20
SCORE_VMEM = 24 * 2**20
RING = 4
WIDTH = 64
QTOK = 256
QUART = 4
ROWS = 2 * WIDTH + 8
TINY = 1e-30
TOP = 15.0


def swap_perm():
    return [(y * 2 + c, y * 2 + 1 - c) for y in range(RING) for c in range(2)]


def y_perm(d):
    return [(y * 2 + c, ((y + d) % RING) * 2 + c) for y in range(RING) for c in range(2)]


def xz_perm(d, flip):
    pairs = []
    for x in range(RING):
        for z in range(RING):
            for t in range(2 * RING):
                along_x = (t % 2 == 0) != flip
                sx, sz = ((x + d) % RING, z) if along_x else (x, (z + d) % RING)
                pairs.append(((sx * RING + sz) * 2 * RING + t, (x * RING + z) * 2 * RING + t))
    return pairs


def add_powers(per, out, j, s):
    for k in range(per):
        for h in range(2):
            most = jnp.max(jnp.abs(out[s * per + k, j, h * WIDTH : (h + 1) * WIDTH, :]), axis=0, keepdims=True)
            power = jnp.ceil(jnp.log2(jnp.maximum(most, TINY)))
            out[s * per + k, j, 2 * WIDTH + 4 * h : 2 * WIDTH + 4 * h + 4, :] = jnp.broadcast_to(power, (4, QTOK))


def project_kernel(chunk, slots, acts, grads, p_in, p_out, keep, give, av, gv, piv, pov, sem_a, sem_g, sem_p):
    t = lax.axis_index("tensor")
    y, core = t // 2, t % 2
    per = chunk // QTOK
    weights, steps = [], []
    order = ((give, 2 * (1 - core), 0), (give, 2 * (1 - core), 1), (keep, 2 * core, 0), (keep, 2 * core, 1))
    for w, (out, first, j) in enumerate(order):
        layer = first + j
        weights.append(
            (
                pltpu.make_async_copy(p_in.at[layer], piv.at[w], sem_p.at[2 * w]),
                pltpu.make_async_copy(p_out.at[layer], pov.at[w], sem_p.at[2 * w + 1]),
            )
        )
        for s in range(QUART // per):
            slot = len(steps) % slots
            group = []
            for k in range(per):
                rows = pl.ds(pl.multiple_of(lax.rem(y + s * per + k, QUART) * QTOK, QTOK), QTOK)
                place = pl.ds(k * QTOK, QTOK)
                group.append(pltpu.make_async_copy(acts.at[layer, rows, :], av.at[slot, place, :], sem_a.at[slot, k]))
                group.append(pltpu.make_async_copy(grads.at[layer, rows, :], gv.at[slot, place, :], sem_g.at[slot, k]))
            steps.append((out, j, s, w, slot, group))
    for n in range(slots):
        if n == 0:
            for c in weights[0]:
                c.start()
        for c in steps[n][5]:
            c.start()
        if n == 0:
            for pair in weights[1:]:
                for c in pair:
                    c.start()
    for n, (out, j, s, w, slot, group) in enumerate(steps):
        if s == 0:
            for c in weights[w]:
                c.wait()
        for c in group:
            c.wait()
        parts = (
            lax.dot_general(piv[w], av[slot], NT, preferred_element_type=jnp.float32),
            lax.dot_general(pov[w], gv[slot], NT, preferred_element_type=jnp.float32),
        )
        if n > 0:
            add_powers(per, *steps[n - 1][:3])
        for h, part in enumerate(parts):
            for k in range(per):
                out[s * per + k, j, h * WIDTH : (h + 1) * WIDTH, :] = part[:, k * QTOK : (k + 1) * QTOK]
        if n + slots < len(steps):
            for c in steps[n + slots][5]:
                c.start()
    add_powers(per, *steps[-1][:3])


def project(acts, grads, p_in, p_out, chunk, slots):
    layers, tokens, d_in, d_out = acts.shape[0], acts.shape[1], acts.shape[2], grads.shape[2]
    in_any = pl.BlockSpec(memory_space=pl.ANY)
    return pl.pallas_call(
        functools.partial(project_kernel, chunk, slots),
        in_specs=[in_any] * 4,
        out_specs=[pl.BlockSpec(memory_space=pltpu.VMEM)] * 2,
        out_shape=[jax.ShapeDtypeStruct((QUART, 2, ROWS, QTOK), jnp.float32)] * 2,
        scratch_shapes=[
            pltpu.VMEM((slots, chunk, d_in), jnp.bfloat16),
            pltpu.VMEM((slots, chunk, d_out), jnp.bfloat16),
            pltpu.VMEM((layers, WIDTH, d_in), jnp.bfloat16),
            pltpu.VMEM((layers, WIDTH, d_out), jnp.bfloat16),
            pltpu.SemaphoreType.DMA((slots, chunk // QTOK)),
            pltpu.SemaphoreType.DMA((slots, chunk // QTOK)),
            pltpu.SemaphoreType.DMA((2 * layers,)),
        ],
        compiler_params=pltpu.CompilerParams(vmem_limit_bytes=PROJECT_VMEM),
        cost_estimate=pl.CostEstimate(
            flops=2 * layers * tokens * (d_in + d_out) * WIDTH,
            bytes_accessed=2 * layers * tokens * (d_in + d_out),
            transcendentals=0,
        ),
        name="project",
    )(acts, grads, p_in, p_out)


def score_kernel(scale, s0, s1, s2, s3, q0, q1, q2a, q2b, q3, keep, give):
    t = lax.axis_index("tensor")
    chip = lax.axis_index("dp")
    y, core = t // 2, t % 2
    x, z = chip // RING, chip % RING
    sums = (s0, s1, s2, s3)

    def query(a, b, j):
        if a == 2:
            return (q2a if b < 2 else q2b)[b % 2, j]
        return (q0, q1, None, q3)[a][b, j]

    for d in range(QUART):
        acc = None
        for j in range(2):
            outs = sums[d][j, WIDTH : 2 * WIDTH, :]
            for a in range(RING):
                for b in range(RING):
                    cx = lax.rem(x + jnp.where(core == 0, b, a), RING)
                    cz = lax.rem(z + jnp.where(core == 0, a, b), RING)
                    base = (cx * RING + cz) * 4
                    feats = jnp.concatenate(
                        [
                            (sums[d][j, pl.ds(base + i, 1), :] * outs).astype(jnp.bfloat16)
                            for i in range(4)
                        ],
                        0,
                    )
                    part = jnp.dot(query(a, b, j), feats, preferred_element_type=jnp.float32)
                    acc = part if acc is None else acc + part
        acc = acc * scale
        place = pl.ds(pl.multiple_of(lax.rem(y + d, QUART) * QTOK, QTOK), QTOK)
        keep[:, place] = acc[0:WIDTH]
        give[:, place] = acc[WIDTH : 2 * WIDTH]


def score(sums, quers, scale):
    vm = pl.BlockSpec(memory_space=pltpu.VMEM)
    shape = jax.ShapeDtypeStruct((WIDTH, QUART * QTOK), jnp.float32)
    return pl.pallas_call(
        functools.partial(score_kernel, scale),
        in_specs=[vm] * 9,
        out_specs=[vm] * 2,
        out_shape=[shape] * 2,
        compiler_params=pltpu.CompilerParams(vmem_limit_bytes=SCORE_VMEM),
        cost_estimate=pl.CostEstimate(
            flops=2 * 2 * 1024 * 4096 * 128, bytes_accessed=4 * 2**20, transcendentals=0
        ),
        name="score",
    )(*sums, *quers)


def row_index():
    return lax.broadcasted_iota(jnp.int32, (1, ROWS, 1), 1)


def powers(message):
    row = row_index()
    first = message[:, 2 * WIDTH : 2 * WIDTH + 1].astype(jnp.float32)
    second = message[:, 2 * WIDTH + 4 : 2 * WIDTH + 5].astype(jnp.float32)
    return jnp.where((row < WIDTH) | ((row >= 2 * WIDTH) & (row < 2 * WIDTH + 4)), first, second)


def pack(values, power):
    scaled = values * jnp.exp2(TOP - power)
    return jnp.where(row_index() < 2 * WIDTH, scaled, power).astype(jnp.float16)


def unpack(message):
    return message.astype(jnp.float32) * jnp.exp2(powers(message) - TOP)


def local(activations, out_grads, proj_input, proj_output, query_feats):
    layers = activations.shape[0]
    width = proj_input.shape[1]
    scale = (layers * width * width) ** (-0.5)
    core = lax.axis_index("tensor") % 2
    both = ("dp", "tensor")

    theirs = lax.ppermute(query_feats, "tensor", swap_perm())
    mine = lax.dynamic_slice_in_dim(query_feats, 2 * core, 2, 0)
    got = lax.dynamic_slice_in_dim(theirs, 2 * core, 2, 0)
    line0 = jnp.concatenate([mine, got], axis=1)
    lines = [line0] + [lax.ppermute(line0, both, xz_perm(d, False)) for d in range(1, RING)]
    keep, give = project(activations, out_grads, proj_input, proj_output, 512, 3)
    give, lines = lax.optimization_barrier((give, lines))
    plane0 = jnp.stack(lines)
    taken = lax.ppermute(give, "tensor", swap_perm())
    part = [keep[d] + taken[d] for d in range(QUART)]
    power = [jnp.maximum(powers(keep[d]), powers(taken[d])) + 1.0 for d in range(QUART)]
    packed = [pack(part[d], power[d]) for d in range(1, QUART)]
    sent = [lax.ppermute(packed[d - 1], "tensor", y_perm(d)) for d in range(1, QUART)]
    plane1 = lax.ppermute(plane0, both, xz_perm(1, True))
    plane3 = lax.ppermute(plane0, both, xz_perm(3, True))
    total = part[0] + sum(unpack(m) for m in sent)
    top = power[0]
    for m in sent:
        top = jnp.maximum(top, powers(m))
    message = pack(total, top + 2.0)
    message, plane1, plane3 = lax.optimization_barrier((message, plane1, plane3))
    plane2 = (
        lax.ppermute(plane1[:2], both, xz_perm(1, True)),
        lax.ppermute(plane3[2:], both, xz_perm(3, True)),
    )
    quers = [plane0, plane1, *plane2, plane3]
    sums = [total[:, : 2 * WIDTH]]
    for d in range(1, QUART):
        sums.append(unpack(lax.ppermute(message, "tensor", y_perm(-d)))[:, : 2 * WIDTH])

    keep_s, give_s = score(sums, quers, scale)
    return (keep_s + lax.ppermute(give_s, "tensor", swap_perm())).T


def solution(mesh):
    in_specs = (
        P(None, "dp", "tensor"),
        P(None, "dp", "tensor"),
        P(None, None, "tensor"),
        P(None, None, "tensor"),
        P(None, "tensor", "dp"),
    )
    out_specs = P("dp", "tensor")
    return jax.shard_map(local, mesh=mesh, in_specs=in_specs, out_specs=out_specs, check_vma=False)
```

```python
import functools

import jax
import jax.numpy as jnp
from jax import lax
from jax.experimental import pallas as pl
from jax.experimental.pallas import tpu as pltpu
from jax.sharding import PartitionSpec as P

NT = (((1,), (1,)), ((), ()))
PROJECT_VMEM = 61 * 2**20
SCORE_VMEM = 24 * 2**20
OWN_FLOPS = 12 * 10**9
RING = 4
WIDTH = 64
QTOK = 256
QUART = 4
ROWS = 2 * WIDTH + 8
TINY = 1e-30
TOP = 15.0


def swap_perm():
    return [(y * 2 + c, y * 2 + 1 - c) for y in range(RING) for c in range(2)]


def y_perm(d):
    return [(y * 2 + c, ((y + d) % RING) * 2 + c) for y in range(RING) for c in range(2)]


def xz_perm(d, flip):
    pairs = []
    for x in range(RING):
        for z in range(RING):
            for t in range(2 * RING):
                along_x = (t % 2 == 0) != flip
                sx, sz = ((x + d) % RING, z) if along_x else (x, (z + d) % RING)
                pairs.append(((sx * RING + sz) * 2 * RING + t, (x * RING + z) * 2 * RING + t))
    return pairs


def add_powers(per, out, j, s):
    for k in range(per):
        for h in range(2):
            most = jnp.max(jnp.abs(out[s * per + k, j, h * WIDTH : (h + 1) * WIDTH, :]), axis=0, keepdims=True)
            power = jnp.ceil(jnp.log2(jnp.maximum(most, TINY)))
            out[s * per + k, j, 2 * WIDTH + 4 * h : 2 * WIDTH + 4 * h + 4, :] = jnp.broadcast_to(power, (4, QTOK))


def project_kernel(chunk, slots, acts, grads, p_in, p_out, keep, give, av, gv, piv, pov, sem_a, sem_g, sem_p):
    t = lax.axis_index("tensor")
    y, core = t // 2, t % 2
    per = chunk // QTOK
    weights, steps = [], []
    order = ((give, 2 * (1 - core), 0), (give, 2 * (1 - core), 1), (keep, 2 * core, 0), (keep, 2 * core, 1))
    for w, (out, first, j) in enumerate(order):
        layer = first + j
        weights.append(
            (
                pltpu.make_async_copy(p_in.at[layer], piv.at[w], sem_p.at[2 * w]),
                pltpu.make_async_copy(p_out.at[layer], pov.at[w], sem_p.at[2 * w + 1]),
            )
        )
        for s in range(QUART // per):
            slot = len(steps) % slots
            group = []
            for k in range(per):
                rows = pl.ds(pl.multiple_of(lax.rem(y + s * per + k, QUART) * QTOK, QTOK), QTOK)
                place = pl.ds(k * QTOK, QTOK)
                group.append(pltpu.make_async_copy(acts.at[layer, rows, :], av.at[slot, place, :], sem_a.at[slot, k]))
                group.append(pltpu.make_async_copy(grads.at[layer, rows, :], gv.at[slot, place, :], sem_g.at[slot, k]))
            steps.append((out, j, s, w, slot, group))
    for n in range(slots):
        if n == 0:
            for c in weights[0]:
                c.start()
        for c in steps[n][5]:
            c.start()
        if n == 0:
            for pair in weights[1:]:
                for c in pair:
                    c.start()
    for n, (out, j, s, w, slot, group) in enumerate(steps):
        if s == 0:
            for c in weights[w]:
                c.wait()
        for c in group:
            c.wait()
        parts = (
            lax.dot_general(piv[w], av[slot], NT, preferred_element_type=jnp.float32),
            lax.dot_general(pov[w], gv[slot], NT, preferred_element_type=jnp.float32),
        )
        if n > 0:
            add_powers(per, *steps[n - 1][:3])
        for h, part in enumerate(parts):
            for k in range(per):
                out[s * per + k, j, h * WIDTH : (h + 1) * WIDTH, :] = part[:, k * QTOK : (k + 1) * QTOK]
        if n + slots < len(steps):
            for c in steps[n + slots][5]:
                c.start()
    add_powers(per, *steps[-1][:3])


def project(acts, grads, p_in, p_out, chunk, slots):
    layers, tokens, d_in, d_out = acts.shape[0], acts.shape[1], acts.shape[2], grads.shape[2]
    in_any = pl.BlockSpec(memory_space=pl.ANY)
    return pl.pallas_call(
        functools.partial(project_kernel, chunk, slots),
        in_specs=[in_any] * 4,
        out_specs=[pl.BlockSpec(memory_space=pltpu.VMEM)] * 2,
        out_shape=[jax.ShapeDtypeStruct((QUART, 2, ROWS, QTOK), jnp.float32)] * 2,
        scratch_shapes=[
            pltpu.VMEM((slots, chunk, d_in), jnp.bfloat16),
            pltpu.VMEM((slots, chunk, d_out), jnp.bfloat16),
            pltpu.VMEM((layers, WIDTH, d_in), jnp.bfloat16),
            pltpu.VMEM((layers, WIDTH, d_out), jnp.bfloat16),
            pltpu.SemaphoreType.DMA((slots, chunk // QTOK)),
            pltpu.SemaphoreType.DMA((slots, chunk // QTOK)),
            pltpu.SemaphoreType.DMA((2 * layers,)),
        ],
        compiler_params=pltpu.CompilerParams(vmem_limit_bytes=PROJECT_VMEM),
        cost_estimate=pl.CostEstimate(
            flops=2 * layers * tokens * (d_in + d_out) * WIDTH,
            bytes_accessed=2 * layers * tokens * (d_in + d_out),
            transcendentals=0,
        ),
        name="project",
    )(acts, grads, p_in, p_out)


def score_tokens(scale, sums, q0, q1, q2a, q2b, q3):
    core = lax.axis_index("tensor") % 2
    chip = lax.axis_index("dp")
    x, z = chip // RING, chip % RING

    def query(a, b, j):
        if a == 2:
            return (q2a if b < 2 else q2b)[b % 2, j]
        return (q0, q1, None, q3)[a][b, j]

    acc = None
    for j in range(2):
        outs = sums[j, WIDTH : 2 * WIDTH, :]
        for a in range(RING):
            for b in range(RING):
                cx = lax.rem(x + jnp.where(core == 0, b, a), RING)
                cz = lax.rem(z + jnp.where(core == 0, a, b), RING)
                base = (cx * RING + cz) * 4
                feats = jnp.concatenate(
                    [(sums[j, pl.ds(base + i, 1), :] * outs).astype(jnp.bfloat16) for i in range(4)], 0
                )
                part = jnp.dot(query(a, b, j), feats, preferred_element_type=jnp.float32)
                acc = part if acc is None else acc + part
    return acc * scale


def own_score_kernel(scale, s0, q0, q1, q2a, q2b, q3, out):
    out[...] = score_tokens(scale, s0, q0, q1, q2a, q2b, q3)


def score_kernel(scale, own, s1, s2, s3, q0, q1, q2a, q2b, q3, keep, give):
    y = lax.axis_index("tensor") // 2
    for d, sums in enumerate((None, s1, s2, s3)):
        acc = own[...] if d == 0 else score_tokens(scale, sums, q0, q1, q2a, q2b, q3)
        place = pl.ds(pl.multiple_of(lax.rem(y + d, QUART) * QTOK, QTOK), QTOK)
        keep[:, place] = acc[0:WIDTH]
        give[:, place] = acc[WIDTH : 2 * WIDTH]


def own_score(total, quers, scale):
    vm = pl.BlockSpec(memory_space=pltpu.VMEM)
    return pl.pallas_call(
        functools.partial(own_score_kernel, scale),
        in_specs=[vm] * 6,
        out_specs=vm,
        out_shape=jax.ShapeDtypeStruct((2 * WIDTH, QTOK), jnp.float32),
        compiler_params=pltpu.CompilerParams(vmem_limit_bytes=SCORE_VMEM),
        cost_estimate=pl.CostEstimate(flops=OWN_FLOPS, bytes_accessed=4 * 2**20, transcendentals=0),
        name="own_score",
    )(total, *quers)


def score(own, sums, quers, scale):
    vm = pl.BlockSpec(memory_space=pltpu.VMEM)
    shape = jax.ShapeDtypeStruct((WIDTH, QUART * QTOK), jnp.float32)
    return pl.pallas_call(
        functools.partial(score_kernel, scale),
        in_specs=[vm] * 9,
        out_specs=[vm] * 2,
        out_shape=[shape] * 2,
        compiler_params=pltpu.CompilerParams(vmem_limit_bytes=SCORE_VMEM),
        cost_estimate=pl.CostEstimate(
            flops=2 * 2 * 1024 * 4096 * 128, bytes_accessed=4 * 2**20, transcendentals=0
        ),
        name="score",
    )(own, *sums, *quers)


def after(value, other):
    return lax.optimization_barrier((value, other))[0]


def row_index():
    return lax.broadcasted_iota(jnp.int32, (1, ROWS, 1), 1)


def powers(message):
    row = row_index()
    first = message[:, 2 * WIDTH : 2 * WIDTH + 1].astype(jnp.float32)
    second = message[:, 2 * WIDTH + 4 : 2 * WIDTH + 5].astype(jnp.float32)
    return jnp.where((row < WIDTH) | ((row >= 2 * WIDTH) & (row < 2 * WIDTH + 4)), first, second)


def pack(values, power):
    scaled = values * jnp.exp2(TOP - power)
    return jnp.where(row_index() < 2 * WIDTH, scaled, power).astype(jnp.float16)


def unpack(message):
    return message.astype(jnp.float32) * jnp.exp2(powers(message) - TOP)


def local(activations, out_grads, proj_input, proj_output, query_feats):
    layers = activations.shape[0]
    width = proj_input.shape[1]
    scale = (layers * width * width) ** (-0.5)
    core = lax.axis_index("tensor") % 2
    both = ("dp", "tensor")

    theirs = lax.ppermute(query_feats, "tensor", swap_perm())
    mine = lax.dynamic_slice_in_dim(query_feats, 2 * core, 2, 0)
    got = lax.dynamic_slice_in_dim(theirs, 2 * core, 2, 0)
    line0 = jnp.concatenate([mine, got], axis=1)
    lines = [line0] + [lax.ppermute(line0, both, xz_perm(d, False)) for d in range(1, RING)]
    keep, give = project(activations, out_grads, proj_input, proj_output, 512, 3)
    give, lines = lax.optimization_barrier((give, lines))
    plane0 = jnp.stack(lines)
    taken = lax.ppermute(give, "tensor", swap_perm())
    part = [keep[d] + taken[d] for d in range(QUART)]
    power = [jnp.maximum(powers(keep[d]), powers(taken[d])) + 1.0 for d in range(QUART)]
    packed = [pack(part[d], power[d]) for d in range(1, QUART)]
    sent = [lax.ppermute(packed[d - 1], "tensor", y_perm(d)) for d in range(1, QUART)]
    plane1 = lax.ppermute(plane0, both, xz_perm(1, True))
    plane3 = lax.ppermute(plane0, both, xz_perm(3, True))
    total = part[0] + sum(unpack(m) for m in sent)
    top = power[0]
    for m in sent:
        top = jnp.maximum(top, powers(m))
    message = pack(total, top + 2.0)
    plane1 = after(plane1, sent[2])
    plane2 = lax.ppermute(plane1, both, xz_perm(1, True))
    plane2 = (plane2[:2], plane2[2:])
    quers = [plane0, plane1, *plane2, plane3]
    own = own_score(total[:, : 2 * WIDTH], quers, scale)
    sums = []
    for d in range(1, QUART):
        sums.append(unpack(after(lax.ppermute(message, "tensor", y_perm(-d)), own))[:, : 2 * WIDTH])

    keep_s, give_s = score(own, sums, quers, scale)
    return (keep_s + lax.ppermute(give_s, "tensor", swap_perm())).T


def solution(mesh):
    in_specs = (
        P(None, "dp", "tensor"),
        P(None, "dp", "tensor"),
        P(None, None, "tensor"),
        P(None, None, "tensor"),
        P(None, "tensor", "dp"),
    )
    out_specs = P("dp", "tensor")
    return jax.shard_map(local, mesh=mesh, in_specs=in_specs, out_specs=out_specs, check_vma=False)
```

```python
import functools

import jax
import jax.numpy as jnp
from jax import lax
from jax.experimental import pallas as pl
from jax.experimental.pallas import tpu as pltpu
from jax.sharding import PartitionSpec as P

NT = (((1,), (1,)), ((), ()))
PROJECT_VMEM = 61 * 2**20
SCORE_VMEM = 24 * 2**20
ORDER = (1, 3, 2)
OWN_FLOPS = 12 * 10**9
RING = 4
WIDTH = 64
QTOK = 256
QUART = 4
ROWS = 2 * WIDTH + 8
TINY = 1e-30
TOP = 15.0


def flip(v, d):
    return (v, v + 1 - 2 * (v % 2), (v + 2) % 4, 3 - v)[d]


def swap_perm():
    return [(y * 2 + c, y * 2 + 1 - c) for y in range(RING) for c in range(2)]


def y_perm(d):
    return [(y * 2 + c, flip(y, d) * 2 + c) for y in range(RING) for c in range(2)]


def xz_perm(d, other):
    pairs = []
    for x in range(RING):
        for z in range(RING):
            for t in range(2 * RING):
                along_x = (t % 2 == 0) != other
                sx, sz = (flip(x, d), z) if along_x else (x, flip(z, d))
                pairs.append(((sx * RING + sz) * 2 * RING + t, (x * RING + z) * 2 * RING + t))
    return pairs


def add_powers(per, out, j, s):
    for k in range(per):
        for h in range(2):
            most = jnp.max(jnp.abs(out[s * per + k, j, h * WIDTH : (h + 1) * WIDTH, :]), axis=0, keepdims=True)
            power = jnp.ceil(jnp.log2(jnp.maximum(most, TINY)))
            out[s * per + k, j, 2 * WIDTH + 4 * h : 2 * WIDTH + 4 * h + 4, :] = jnp.broadcast_to(power, (4, QTOK))


def project_kernel(chunk, slots, acts, grads, p_in, p_out, keep, give, av, gv, piv, pov, sem_a, sem_g, sem_p):
    t = lax.axis_index("tensor")
    y, core = t // 2, t % 2
    per = chunk // QTOK
    weights, steps = [], []
    order = ((give, 2 * (1 - core), 0), (give, 2 * (1 - core), 1), (keep, 2 * core, 0), (keep, 2 * core, 1))
    for w, (out, first, j) in enumerate(order):
        layer = first + j
        weights.append(
            (
                pltpu.make_async_copy(p_in.at[layer], piv.at[w], sem_p.at[2 * w]),
                pltpu.make_async_copy(p_out.at[layer], pov.at[w], sem_p.at[2 * w + 1]),
            )
        )
        for s in range(QUART // per):
            slot = len(steps) % slots
            group = []
            for k in range(per):
                rows = pl.ds(pl.multiple_of(flip(y, s * per + k) * QTOK, QTOK), QTOK)
                place = pl.ds(k * QTOK, QTOK)
                group.append(pltpu.make_async_copy(acts.at[layer, rows, :], av.at[slot, place, :], sem_a.at[slot, k]))
                group.append(pltpu.make_async_copy(grads.at[layer, rows, :], gv.at[slot, place, :], sem_g.at[slot, k]))
            steps.append((out, j, s, w, slot, group))
    for n in range(slots):
        if n == 0:
            for c in weights[0]:
                c.start()
        for c in steps[n][5]:
            c.start()
        if n == 0:
            for pair in weights[1:]:
                for c in pair:
                    c.start()
    for n, (out, j, s, w, slot, group) in enumerate(steps):
        if s == 0:
            for c in weights[w]:
                c.wait()
        for c in group:
            c.wait()
        parts = (
            lax.dot_general(piv[w], av[slot], NT, preferred_element_type=jnp.float32),
            lax.dot_general(pov[w], gv[slot], NT, preferred_element_type=jnp.float32),
        )
        if n > 0:
            add_powers(per, *steps[n - 1][:3])
        for h, part in enumerate(parts):
            for k in range(per):
                out[s * per + k, j, h * WIDTH : (h + 1) * WIDTH, :] = part[:, k * QTOK : (k + 1) * QTOK]
        if n + slots < len(steps):
            for c in steps[n + slots][5]:
                c.start()
    add_powers(per, *steps[-1][:3])


def project(acts, grads, p_in, p_out, chunk, slots):
    layers, tokens, d_in, d_out = acts.shape[0], acts.shape[1], acts.shape[2], grads.shape[2]
    in_any = pl.BlockSpec(memory_space=pl.ANY)
    return pl.pallas_call(
        functools.partial(project_kernel, chunk, slots),
        in_specs=[in_any] * 4,
        out_specs=[pl.BlockSpec(memory_space=pltpu.VMEM)] * 2,
        out_shape=[jax.ShapeDtypeStruct((QUART, 2, ROWS, QTOK), jnp.float32)] * 2,
        scratch_shapes=[
            pltpu.VMEM((slots, chunk, d_in), jnp.bfloat16),
            pltpu.VMEM((slots, chunk, d_out), jnp.bfloat16),
            pltpu.VMEM((layers, WIDTH, d_in), jnp.bfloat16),
            pltpu.VMEM((layers, WIDTH, d_out), jnp.bfloat16),
            pltpu.SemaphoreType.DMA((slots, chunk // QTOK)),
            pltpu.SemaphoreType.DMA((slots, chunk // QTOK)),
            pltpu.SemaphoreType.DMA((2 * layers,)),
        ],
        compiler_params=pltpu.CompilerParams(vmem_limit_bytes=PROJECT_VMEM),
        cost_estimate=pl.CostEstimate(
            flops=2 * layers * tokens * (d_in + d_out) * WIDTH,
            bytes_accessed=2 * layers * tokens * (d_in + d_out),
            transcendentals=0,
        ),
        name="project",
    )(acts, grads, p_in, p_out)


def score_tokens(scale, sums, q0, q1, q2a, q2b, q3):
    core = lax.axis_index("tensor") % 2
    chip = lax.axis_index("dp")
    x, z = chip // RING, chip % RING

    def query(a, b, j):
        if a == 2:
            return (q2a if b < 2 else q2b)[b % 2, j]
        return (q0, q1, None, q3)[a][b, j]

    acc = None
    for j in range(2):
        outs = sums[j, WIDTH : 2 * WIDTH, :]
        for a in range(RING):
            for b in range(RING):
                cx = jnp.where(core == 0, flip(x, b), flip(x, a))
                cz = jnp.where(core == 0, flip(z, a), flip(z, b))
                base = (cx * RING + cz) * 4
                feats = jnp.concatenate(
                    [(sums[j, pl.ds(base + i, 1), :] * outs).astype(jnp.bfloat16) for i in range(4)], 0
                )
                part = jnp.dot(query(a, b, j), feats, preferred_element_type=jnp.float32)
                acc = part if acc is None else acc + part
    return acc * scale


def own_score_kernel(scale, s0, q0, q1, q2a, q2b, q3, out):
    out[...] = score_tokens(scale, s0, q0, q1, q2a, q2b, q3)


def score_kernel(scale, own, s1, s2, s3, q0, q1, q2a, q2b, q3, keep, give):
    y = lax.axis_index("tensor") // 2
    for d, sums in enumerate((None, s1, s2, s3)):
        acc = own[...] if d == 0 else score_tokens(scale, sums, q0, q1, q2a, q2b, q3)
        place = pl.ds(pl.multiple_of(flip(y, d) * QTOK, QTOK), QTOK)
        keep[:, place] = acc[0:WIDTH]
        give[:, place] = acc[WIDTH : 2 * WIDTH]


def own_score(total, quers, scale):
    vm = pl.BlockSpec(memory_space=pltpu.VMEM)
    return pl.pallas_call(
        functools.partial(own_score_kernel, scale),
        in_specs=[vm] * 6,
        out_specs=vm,
        out_shape=jax.ShapeDtypeStruct((2 * WIDTH, QTOK), jnp.float32),
        compiler_params=pltpu.CompilerParams(vmem_limit_bytes=SCORE_VMEM),
        cost_estimate=pl.CostEstimate(flops=OWN_FLOPS, bytes_accessed=4 * 2**20, transcendentals=0),
        name="own_score",
    )(total, *quers)


def score(own, sums, quers, scale):
    vm = pl.BlockSpec(memory_space=pltpu.VMEM)
    shape = jax.ShapeDtypeStruct((WIDTH, QUART * QTOK), jnp.float32)
    return pl.pallas_call(
        functools.partial(score_kernel, scale),
        in_specs=[vm] * 9,
        out_specs=[vm] * 2,
        out_shape=[shape] * 2,
        compiler_params=pltpu.CompilerParams(vmem_limit_bytes=SCORE_VMEM),
        cost_estimate=pl.CostEstimate(
            flops=2 * 2 * 1024 * 4096 * 128, bytes_accessed=4 * 2**20, transcendentals=0
        ),
        name="score",
    )(own, *sums, *quers)


def after(value, other):
    return lax.optimization_barrier((value, other))[0]


def row_index():
    return lax.broadcasted_iota(jnp.int32, (1, ROWS, 1), 1)


def powers(message):
    row = row_index()
    first = message[:, 2 * WIDTH : 2 * WIDTH + 1].astype(jnp.float32)
    second = message[:, 2 * WIDTH + 4 : 2 * WIDTH + 5].astype(jnp.float32)
    return jnp.where((row < WIDTH) | ((row >= 2 * WIDTH) & (row < 2 * WIDTH + 4)), first, second)


def pack(values, power):
    scaled = values * jnp.exp2(TOP - power)
    return jnp.where(row_index() < 2 * WIDTH, scaled, power).astype(jnp.float16)


def unpack(message):
    return message.astype(jnp.float32) * jnp.exp2(powers(message) - TOP)


def local(activations, out_grads, proj_input, proj_output, query_feats):
    layers = activations.shape[0]
    width = proj_input.shape[1]
    scale = (layers * width * width) ** (-0.5)
    core = lax.axis_index("tensor") % 2
    both = ("dp", "tensor")

    theirs = lax.ppermute(query_feats, "tensor", swap_perm())
    mine = lax.dynamic_slice_in_dim(query_feats, 2 * core, 2, 0)
    got = lax.dynamic_slice_in_dim(theirs, 2 * core, 2, 0)
    line0 = jnp.concatenate([mine, got], axis=1)
    lines = [line0] + [lax.ppermute(line0, both, xz_perm(d, False)) for d in range(1, RING)]
    keep, give = project(activations, out_grads, proj_input, proj_output, 512, 3)
    give, lines = lax.optimization_barrier((give, lines))
    plane0 = jnp.stack(lines)
    taken = lax.ppermute(give, "tensor", swap_perm())
    part = [keep[d] + taken[d] for d in range(QUART)]
    power = [jnp.maximum(powers(keep[d]), powers(taken[d])) + 1.0 for d in range(QUART)]
    packed = [pack(part[d], power[d]) for d in range(1, QUART)]
    sent = [None] * 3
    for d in ORDER:
        sent[d - 1] = lax.ppermute(packed[d - 1], "tensor", y_perm(d))
    plane1 = lax.ppermute(plane0, both, xz_perm(1, True))
    plane3 = lax.ppermute(plane0, both, xz_perm(3, True))
    total = part[0] + sum(unpack(m) for m in sent)
    top = power[0]
    for m in sent:
        top = jnp.maximum(top, powers(m))
    message = pack(total, top + 2.0)
    plane3 = after(plane3, sent[1])
    plane2 = lax.ppermute(plane3, both, xz_perm(1, True))
    plane2 = (plane2[:2], plane2[2:])
    quers = [plane0, plane1, *plane2, plane3]
    own = own_score(total[:, : 2 * WIDTH], quers, scale)
    sums = [None] * 3
    for d in ORDER:
        sums[d - 1] = unpack(after(lax.ppermute(message, "tensor", y_perm(d)), own))[:, : 2 * WIDTH]

    keep_s, give_s = score(own, sums, quers, scale)
    return (keep_s + lax.ppermute(give_s, "tensor", swap_perm())).T


def solution(mesh):
    in_specs = (
        P(None, "dp", "tensor"),
        P(None, "dp", "tensor"),
        P(None, None, "tensor"),
        P(None, None, "tensor"),
        P(None, "tensor", "dp"),
    )
    out_specs = P("dp", "tensor")
    return jax.shard_map(local, mesh=mesh, in_specs=in_specs, out_specs=out_specs, check_vma=False)
```

```python
import functools

import jax
import jax.numpy as jnp
from jax import lax
from jax.experimental import pallas as pl
from jax.experimental.pallas import tpu as pltpu
from jax.sharding import PartitionSpec as P

NT = (((1,), (1,)), ((), ()))
PROJECT_VMEM = 61 * 2**20
SCORE_VMEM = 24 * 2**20
ORDER = (1, 3, 2)
OWN_FLOPS = 12 * 10**9
RING = 4
WIDTH = 64
QTOK = 256
QUART = 4
ROWS = 2 * WIDTH + 8
TINY = 1e-30
TOP = 15.0


def flip(v, d):
    return (v, v + 1 - 2 * (v % 2), (v + 2) % 4, 3 - v)[d]


def swap_perm():
    return [(y * 2 + c, y * 2 + 1 - c) for y in range(RING) for c in range(2)]


def y_perm(d):
    return [(y * 2 + c, flip(y, d) * 2 + c) for y in range(RING) for c in range(2)]


def xz_perm(d, other):
    pairs = []
    for x in range(RING):
        for z in range(RING):
            for t in range(2 * RING):
                along_x = (t % 2 == 0) != other
                sx, sz = (flip(x, d), z) if along_x else (x, flip(z, d))
                pairs.append(((sx * RING + sz) * 2 * RING + t, (x * RING + z) * 2 * RING + t))
    return pairs


def add_powers(per, out, j, s):
    for k in range(per):
        for h in range(2):
            most = jnp.max(jnp.abs(out[s * per + k, j, h * WIDTH : (h + 1) * WIDTH, :]), axis=0, keepdims=True)
            power = jnp.ceil(jnp.log2(jnp.maximum(most, TINY)))
            out[s * per + k, j, 2 * WIDTH + 4 * h : 2 * WIDTH + 4 * h + 4, :] = jnp.broadcast_to(power, (4, QTOK))


def project_kernel(chunk, slots, acts, grads, p_in, p_out, keep, give, av, gv, piv, pov, sem_a, sem_g, sem_p):
    t = lax.axis_index("tensor")
    y, core = t // 2, t % 2
    per = chunk // QTOK
    weights, steps = [], []
    order = ((give, 2 * (1 - core), 0), (give, 2 * (1 - core), 1), (keep, 2 * core, 0), (keep, 2 * core, 1))
    for w, (out, first, j) in enumerate(order):
        layer = first + j
        weights.append(
            (
                pltpu.make_async_copy(p_in.at[layer], piv.at[w], sem_p.at[2 * w]),
                pltpu.make_async_copy(p_out.at[layer], pov.at[w], sem_p.at[2 * w + 1]),
            )
        )
        for s in range(QUART // per):
            slot = len(steps) % slots
            group = []
            for k in range(per):
                rows = pl.ds(pl.multiple_of(flip(y, s * per + k) * QTOK, QTOK), QTOK)
                place = pl.ds(k * QTOK, QTOK)
                group.append(pltpu.make_async_copy(acts.at[layer, rows, :], av.at[slot, place, :], sem_a.at[slot, k]))
                group.append(pltpu.make_async_copy(grads.at[layer, rows, :], gv.at[slot, place, :], sem_g.at[slot, k]))
            steps.append((out, j, s, w, slot, group))
    for n in range(slots):
        if n == 0:
            for c in weights[0]:
                c.start()
        for c in steps[n][5]:
            c.start()
        if n == 0:
            for pair in weights[1:]:
                for c in pair:
                    c.start()
    for n, (out, j, s, w, slot, group) in enumerate(steps):
        if s == 0:
            for c in weights[w]:
                c.wait()
        for c in group:
            c.wait()
        parts = (
            lax.dot_general(piv[w], av[slot], NT, preferred_element_type=jnp.float32),
            lax.dot_general(pov[w], gv[slot], NT, preferred_element_type=jnp.float32),
        )
        if n > 0:
            add_powers(per, *steps[n - 1][:3])
        for h, part in enumerate(parts):
            for k in range(per):
                out[s * per + k, j, h * WIDTH : (h + 1) * WIDTH, :] = part[:, k * QTOK : (k + 1) * QTOK]
        if n + slots < len(steps):
            for c in steps[n + slots][5]:
                c.start()
    add_powers(per, *steps[-1][:3])


def project(acts, grads, p_in, p_out, chunk, slots):
    layers, tokens, d_in, d_out = acts.shape[0], acts.shape[1], acts.shape[2], grads.shape[2]
    in_any = pl.BlockSpec(memory_space=pl.ANY)
    return pl.pallas_call(
        functools.partial(project_kernel, chunk, slots),
        in_specs=[in_any] * 4,
        out_specs=[pl.BlockSpec(memory_space=pltpu.VMEM)] * 2,
        out_shape=[jax.ShapeDtypeStruct((QUART, 2, ROWS, QTOK), jnp.float32)] * 2,
        scratch_shapes=[
            pltpu.VMEM((slots, chunk, d_in), jnp.bfloat16),
            pltpu.VMEM((slots, chunk, d_out), jnp.bfloat16),
            pltpu.VMEM((layers, WIDTH, d_in), jnp.bfloat16),
            pltpu.VMEM((layers, WIDTH, d_out), jnp.bfloat16),
            pltpu.SemaphoreType.DMA((slots, chunk // QTOK)),
            pltpu.SemaphoreType.DMA((slots, chunk // QTOK)),
            pltpu.SemaphoreType.DMA((2 * layers,)),
        ],
        compiler_params=pltpu.CompilerParams(vmem_limit_bytes=PROJECT_VMEM),
        cost_estimate=pl.CostEstimate(
            flops=2 * layers * tokens * (d_in + d_out) * WIDTH,
            bytes_accessed=2 * layers * tokens * (d_in + d_out),
            transcendentals=0,
        ),
        name="project",
    )(acts, grads, p_in, p_out)


def score_tokens(scale, sums, q0, q1, q3, q2):
    core = lax.axis_index("tensor") % 2
    chip = lax.axis_index("dp")
    x, z = chip // RING, chip % RING

    def query(a, b, j):
        return (q0, q1, q2, q3)[a][b, j]

    acc = None
    for j in range(2):
        outs = sums[j, WIDTH : 2 * WIDTH, :]
        for a in range(RING):
            for b in range(RING):
                cx = jnp.where(core == 0, flip(x, b), flip(x, a))
                cz = jnp.where(core == 0, flip(z, a), flip(z, b))
                base = (cx * RING + cz) * 4
                feats = jnp.concatenate(
                    [(sums[j, pl.ds(base + i, 1), :] * outs).astype(jnp.bfloat16) for i in range(4)], 0
                )
                part = jnp.dot(query(a, b, j), feats, preferred_element_type=jnp.float32)
                acc = part if acc is None else acc + part
    return acc * scale


def own_score_kernel(scale, s0, q0, q1, q3, q2, out):
    out[...] = score_tokens(scale, s0, q0, q1, q3, q2)


def score_kernel(scale, own, s1, s2, s3, q0, q1, q3, q2, keep, give):
    y = lax.axis_index("tensor") // 2
    for d, sums in enumerate((None, s1, s2, s3)):
        acc = own[...] if d == 0 else score_tokens(scale, sums, q0, q1, q3, q2)
        place = pl.ds(pl.multiple_of(flip(y, d) * QTOK, QTOK), QTOK)
        keep[:, place] = acc[0:WIDTH]
        give[:, place] = acc[WIDTH : 2 * WIDTH]


def own_score(total, quers, scale):
    vm = pl.BlockSpec(memory_space=pltpu.VMEM)
    return pl.pallas_call(
        functools.partial(own_score_kernel, scale),
        in_specs=[vm] * 5,
        out_specs=vm,
        out_shape=jax.ShapeDtypeStruct((2 * WIDTH, QTOK), jnp.float32),
        compiler_params=pltpu.CompilerParams(vmem_limit_bytes=SCORE_VMEM),
        cost_estimate=pl.CostEstimate(flops=OWN_FLOPS, bytes_accessed=4 * 2**20, transcendentals=0),
        name="own_score",
    )(total, *quers)


def score(own, sums, quers, scale):
    vm = pl.BlockSpec(memory_space=pltpu.VMEM)
    shape = jax.ShapeDtypeStruct((WIDTH, QUART * QTOK), jnp.float32)
    return pl.pallas_call(
        functools.partial(score_kernel, scale),
        in_specs=[vm] * 8,
        out_specs=[vm] * 2,
        out_shape=[shape] * 2,
        compiler_params=pltpu.CompilerParams(vmem_limit_bytes=SCORE_VMEM),
        cost_estimate=pl.CostEstimate(
            flops=2 * 2 * 1024 * 4096 * 128, bytes_accessed=4 * 2**20, transcendentals=0
        ),
        name="score",
    )(own, *sums, *quers)


def after(value, other):
    return lax.optimization_barrier((value, other))[0]


def row_index():
    return lax.broadcasted_iota(jnp.int32, (1, ROWS, 1), 1)


def powers(message):
    row = row_index()
    first = message[:, 2 * WIDTH : 2 * WIDTH + 1].astype(jnp.float32)
    second = message[:, 2 * WIDTH + 4 : 2 * WIDTH + 5].astype(jnp.float32)
    return jnp.where((row < WIDTH) | ((row >= 2 * WIDTH) & (row < 2 * WIDTH + 4)), first, second)


def pack(values, power):
    scaled = values * jnp.exp2(TOP - power)
    return jnp.where(row_index() < 2 * WIDTH, scaled, power).astype(jnp.float16)


def unpack(message):
    return message.astype(jnp.float32) * jnp.exp2(powers(message) - TOP)


def local(activations, out_grads, proj_input, proj_output, query_feats):
    layers = activations.shape[0]
    width = proj_input.shape[1]
    scale = (layers * width * width) ** (-0.5)
    core = lax.axis_index("tensor") % 2
    both = ("dp", "tensor")

    theirs = lax.ppermute(query_feats, "tensor", swap_perm())
    mine = lax.dynamic_slice_in_dim(query_feats, 2 * core, 2, 0)
    got = lax.dynamic_slice_in_dim(theirs, 2 * core, 2, 0)
    line0 = jnp.concatenate([mine, got], axis=1)
    lines = [line0] + [lax.ppermute(line0, both, xz_perm(d, False)) for d in range(1, RING)]
    keep, give = project(activations, out_grads, proj_input, proj_output, 512, 3)
    give, lines = lax.optimization_barrier((give, lines))
    plane0 = jnp.stack(lines)
    taken = lax.ppermute(give, "tensor", swap_perm())
    part = [keep[d] + taken[d] for d in range(QUART)]
    power = [jnp.maximum(powers(keep[d]), powers(taken[d])) + 1.0 for d in range(QUART)]
    packed = [pack(part[d], power[d]) for d in range(1, QUART)]
    sent = [None] * 3
    for d in ORDER:
        sent[d - 1] = lax.ppermute(packed[d - 1], "tensor", y_perm(d))
    plane1 = lax.ppermute(plane0, both, xz_perm(1, True))
    total = part[0] + sum(unpack(m) for m in sent)
    top = power[0]
    for m in sent:
        top = jnp.maximum(top, powers(m))
    message = pack(total, top + 2.0)
    late = [lax.ppermute(p, both, xz_perm(3, True)) for p in (after(plane0, packed[2]), after(plane1, sent[1]))]
    quers = [plane0, plane1, *late]
    own = own_score(total[:, : 2 * WIDTH], quers, scale)
    sums = [None] * 3
    for d in ORDER:
        sums[d - 1] = unpack(after(lax.ppermute(message, "tensor", y_perm(d)), own))[:, : 2 * WIDTH]

    keep_s, give_s = score(own, sums, quers, scale)
    return (keep_s + lax.ppermute(give_s, "tensor", swap_perm())).T


def solution(mesh):
    in_specs = (
        P(None, "dp", "tensor"),
        P(None, "dp", "tensor"),
        P(None, None, "tensor"),
        P(None, None, "tensor"),
        P(None, "tensor", "dp"),
    )
    out_specs = P("dp", "tensor")
    return jax.shard_map(local, mesh=mesh, in_specs=in_specs, out_specs=out_specs, check_vma=False)
```

```python
import functools

import jax
import jax.numpy as jnp
from jax import lax
from jax.experimental import pallas as pl
from jax.experimental.pallas import tpu as pltpu
from jax.sharding import PartitionSpec as P

NT = (((1,), (1,)), ((), ()))
PROJECT_VMEM = 50 * 2**20
SCORE_VMEM = 24 * 2**20
ORDER = (1, 3, 2)
OWN_FLOPS = 12 * 10**9
RING = 4
WIDTH = 64
QTOK = 256
QUART = 4
ROWS = 2 * WIDTH + 8
TINY = 1e-30
TOP = 15.0


def flip(v, d):
    return (v, v + 1 - 2 * (v % 2), (v + 2) % 4, 3 - v)[d]


def swap_perm():
    return [(y * 2 + c, y * 2 + 1 - c) for y in range(RING) for c in range(2)]


def y_perm(d):
    return [(y * 2 + c, flip(y, d) * 2 + c) for y in range(RING) for c in range(2)]


def xz_perm(d, other):
    pairs = []
    for x in range(RING):
        for z in range(RING):
            for t in range(2 * RING):
                along_x = (t % 2 == 0) != other
                sx, sz = (flip(x, d), z) if along_x else (x, flip(z, d))
                pairs.append(((sx * RING + sz) * 2 * RING + t, (x * RING + z) * 2 * RING + t))
    return pairs


def add_powers(per, out, j, s):
    for k in range(per):
        for h in range(2):
            most = jnp.max(jnp.abs(out[s * per + k, j, h * WIDTH : (h + 1) * WIDTH, :]), axis=0, keepdims=True)
            power = jnp.ceil(jnp.log2(jnp.maximum(most, TINY)))
            out[s * per + k, j, 2 * WIDTH + 4 * h : 2 * WIDTH + 4 * h + 4, :] = jnp.broadcast_to(power, (4, QTOK))


def project_kernel(chunk, slots, acts, grads, proj, keep, give, av, gv, pv, sem_a, sem_g, sem_p):
    t = lax.axis_index("tensor")
    y, core = t // 2, t % 2
    per = chunk // QTOK
    d_in = acts.shape[2]
    weights, steps = [], []
    order = ((give, 2 * (1 - core), 0), (give, 2 * (1 - core), 1), (keep, 2 * core, 0), (keep, 2 * core, 1))
    for w, (out, first, j) in enumerate(order):
        layer = first + j
        weights.append(pltpu.make_async_copy(proj.at[layer], pv.at[w], sem_p.at[w]))
        for s in range(QUART // per):
            slot = len(steps) % slots
            group = []
            for k in range(per):
                rows = pl.ds(pl.multiple_of(flip(y, s * per + k) * QTOK, QTOK), QTOK)
                place = pl.ds(k * QTOK, QTOK)
                group.append(pltpu.make_async_copy(acts.at[layer, rows, :], av.at[slot, place, :], sem_a.at[slot, k]))
                group.append(pltpu.make_async_copy(grads.at[layer, rows, :], gv.at[slot, place, :], sem_g.at[slot, k]))
            steps.append((out, j, s, w, slot, group))
    for n in range(slots):
        if n == 0:
            weights[0].start()
        for c in steps[n][5]:
            c.start()
        if n == 0:
            for c in weights[1:]:
                c.start()
    for n, (out, j, s, w, slot, group) in enumerate(steps):
        if s == 0:
            weights[w].wait()
        for c in group:
            c.wait()
        parts = (
            lax.dot_general(pv[w, :, :d_in], av[slot], NT, preferred_element_type=jnp.float32),
            lax.dot_general(pv[w, :, d_in:], gv[slot], NT, preferred_element_type=jnp.float32),
        )
        if n > 0:
            add_powers(per, *steps[n - 1][:3])
        for h, part in enumerate(parts):
            for k in range(per):
                out[s * per + k, j, h * WIDTH : (h + 1) * WIDTH, :] = part[:, k * QTOK : (k + 1) * QTOK]
        if n + slots < len(steps):
            for c in steps[n + slots][5]:
                c.start()
    add_powers(per, *steps[-1][:3])


def project(acts, grads, proj, chunk, slots):
    layers, tokens, d_in, d_out = acts.shape[0], acts.shape[1], acts.shape[2], grads.shape[2]
    in_any = pl.BlockSpec(memory_space=pl.ANY)
    return pl.pallas_call(
        functools.partial(project_kernel, chunk, slots),
        in_specs=[in_any] * 3,
        out_specs=[pl.BlockSpec(memory_space=pltpu.VMEM)] * 2,
        out_shape=[jax.ShapeDtypeStruct((QUART, 2, ROWS, QTOK), jnp.float32)] * 2,
        scratch_shapes=[
            pltpu.VMEM((slots, chunk, d_in), jnp.bfloat16),
            pltpu.VMEM((slots, chunk, d_out), jnp.bfloat16),
            pltpu.VMEM((layers, WIDTH, d_in + d_out), jnp.bfloat16),
            pltpu.SemaphoreType.DMA((slots, chunk // QTOK)),
            pltpu.SemaphoreType.DMA((slots, chunk // QTOK)),
            pltpu.SemaphoreType.DMA((layers,)),
        ],
        compiler_params=pltpu.CompilerParams(vmem_limit_bytes=PROJECT_VMEM),
        cost_estimate=pl.CostEstimate(
            flops=2 * layers * tokens * (d_in + d_out) * WIDTH,
            bytes_accessed=2 * layers * tokens * (d_in + d_out),
            transcendentals=0,
        ),
        name="project",
    )(acts, grads, proj)


def score_tokens(scale, sums, q0, q1, q3, q2):
    core = lax.axis_index("tensor") % 2
    chip = lax.axis_index("dp")
    x, z = chip // RING, chip % RING

    def query(a, b, j):
        return (q0, q1, q2, q3)[a][b, j]

    acc = None
    for j in range(2):
        outs = sums[j, WIDTH : 2 * WIDTH, :]
        for a in range(RING):
            for b in range(RING):
                cx = jnp.where(core == 0, flip(x, b), flip(x, a))
                cz = jnp.where(core == 0, flip(z, a), flip(z, b))
                base = (cx * RING + cz) * 4
                feats = jnp.concatenate(
                    [(sums[j, pl.ds(base + i, 1), :] * outs).astype(jnp.bfloat16) for i in range(4)], 0
                )
                part = jnp.dot(query(a, b, j), feats, preferred_element_type=jnp.float32)
                acc = part if acc is None else acc + part
    return acc * scale


def own_score_kernel(scale, s0, q0, q1, q3, q2, out):
    out[...] = score_tokens(scale, s0, q0, q1, q3, q2)


def score_kernel(scale, own, s1, s2, s3, q0, q1, q3, q2, keep, give):
    y = lax.axis_index("tensor") // 2
    for d, sums in enumerate((None, s1, s2, s3)):
        acc = own[...] if d == 0 else score_tokens(scale, sums, q0, q1, q3, q2)
        place = pl.ds(pl.multiple_of(flip(y, d) * QTOK, QTOK), QTOK)
        keep[:, place] = acc[0:WIDTH]
        give[:, place] = acc[WIDTH : 2 * WIDTH]


def own_score(total, quers, scale):
    vm = pl.BlockSpec(memory_space=pltpu.VMEM)
    return pl.pallas_call(
        functools.partial(own_score_kernel, scale),
        in_specs=[vm] * 5,
        out_specs=vm,
        out_shape=jax.ShapeDtypeStruct((2 * WIDTH, QTOK), jnp.float32),
        compiler_params=pltpu.CompilerParams(vmem_limit_bytes=SCORE_VMEM),
        cost_estimate=pl.CostEstimate(flops=OWN_FLOPS, bytes_accessed=4 * 2**20, transcendentals=0),
        name="own_score",
    )(total, *quers)


def score(own, sums, quers, scale):
    vm = pl.BlockSpec(memory_space=pltpu.VMEM)
    shape = jax.ShapeDtypeStruct((WIDTH, QUART * QTOK), jnp.float32)
    return pl.pallas_call(
        functools.partial(score_kernel, scale),
        in_specs=[vm] * 8,
        out_specs=[vm] * 2,
        out_shape=[shape] * 2,
        compiler_params=pltpu.CompilerParams(vmem_limit_bytes=SCORE_VMEM),
        cost_estimate=pl.CostEstimate(
            flops=2 * 2 * 1024 * 4096 * 128, bytes_accessed=4 * 2**20, transcendentals=0
        ),
        name="score",
    )(own, *sums, *quers)


def after(value, other):
    return lax.optimization_barrier((value, other))[0]


def row_index():
    return lax.broadcasted_iota(jnp.int32, (1, ROWS, 1), 1)


def powers(message):
    row = row_index()
    first = message[:, 2 * WIDTH : 2 * WIDTH + 1].astype(jnp.float32)
    second = message[:, 2 * WIDTH + 4 : 2 * WIDTH + 5].astype(jnp.float32)
    return jnp.where((row < WIDTH) | ((row >= 2 * WIDTH) & (row < 2 * WIDTH + 4)), first, second)


def pack(values, power):
    scaled = values * jnp.exp2(TOP - power)
    return jnp.where(row_index() < 2 * WIDTH, scaled, power).astype(jnp.float16)


def unpack(message):
    return message.astype(jnp.float32) * jnp.exp2(powers(message) - TOP)


def local(activations, out_grads, proj_input, proj_output, query_feats):
    layers = activations.shape[0]
    width = proj_input.shape[1]
    scale = (layers * width * width) ** (-0.5)
    core = lax.axis_index("tensor") % 2
    both = ("dp", "tensor")

    theirs = lax.ppermute(query_feats, "tensor", swap_perm())
    mine = lax.dynamic_slice_in_dim(query_feats, 2 * core, 2, 0)
    got = lax.dynamic_slice_in_dim(theirs, 2 * core, 2, 0)
    proj = jnp.concatenate([proj_input, proj_output], axis=2)
    line0 = after(jnp.concatenate([mine, got], axis=1), proj)
    lines = [line0] + [lax.ppermute(line0, both, xz_perm(d, False)) for d in range(1, RING)]
    keep, give = project(activations, out_grads, proj, 512, 3)
    give, lines = lax.optimization_barrier((give, lines))
    plane0 = jnp.stack(lines)
    taken = lax.ppermute(give, "tensor", swap_perm())
    part = [keep[d] + taken[d] for d in range(QUART)]
    power = [jnp.maximum(powers(keep[d]), powers(taken[d])) + 1.0 for d in range(QUART)]
    packed = [pack(part[d], power[d]) for d in range(1, QUART)]
    sent = [None] * 3
    for d in ORDER:
        sent[d - 1] = lax.ppermute(packed[d - 1], "tensor", y_perm(d))
    plane1 = lax.ppermute(plane0, both, xz_perm(1, True))
    total = part[0] + sum(unpack(m) for m in sent)
    top = power[0]
    for m in sent:
        top = jnp.maximum(top, powers(m))
    message = pack(total, top + 2.0)
    late = [lax.ppermute(p, both, xz_perm(3, True)) for p in (after(plane0, packed[2]), after(plane1, sent[1]))]
    quers = [plane0, plane1, *late]
    own = own_score(total[:, : 2 * WIDTH], quers, scale)
    sums = [None] * 3
    for d in ORDER:
        sums[d - 1] = unpack(after(lax.ppermute(message, "tensor", y_perm(d)), own))[:, : 2 * WIDTH]

    keep_s, give_s = score(own, sums, quers, scale)
    return (keep_s + lax.ppermute(give_s, "tensor", swap_perm())).T


def solution(mesh):
    in_specs = (
        P(None, "dp", "tensor"),
        P(None, "dp", "tensor"),
        P(None, None, "tensor"),
        P(None, None, "tensor"),
        P(None, "tensor", "dp"),
    )
    out_specs = P("dp", "tensor")
    return jax.shard_map(local, mesh=mesh, in_specs=in_specs, out_specs=out_specs, check_vma=False)
```

```python
import functools

import jax
import jax.numpy as jnp
from jax import lax
from jax.experimental import pallas as pl
from jax.experimental.pallas import tpu as pltpu
from jax.sharding import PartitionSpec as P

NT = (((1,), (1,)), ((), ()))
PROJECT_VMEM = 50 * 2**20
SCORE_VMEM = 24 * 2**20
ORDER = (1, 3, 2)
OWN_FLOPS = 12 * 10**9
RING = 4
WIDTH = 64
QTOK = 256
QUART = 4
ROWS = 2 * WIDTH + 8
TINY = 1e-30
TOP = 15.0


def flip(v, d):
    return (v, v + 1 - 2 * (v % 2), (v + 2) % 4, 3 - v)[d]


def swap_perm():
    return [(y * 2 + c, y * 2 + 1 - c) for y in range(RING) for c in range(2)]


def y_perm(d):
    return [(y * 2 + c, flip(y, d) * 2 + c) for y in range(RING) for c in range(2)]


def xz_perm(d, other):
    pairs = []
    for x in range(RING):
        for z in range(RING):
            for t in range(2 * RING):
                along_x = (t % 2 == 0) != other
                sx, sz = (flip(x, d), z) if along_x else (x, flip(z, d))
                pairs.append(((sx * RING + sz) * 2 * RING + t, (x * RING + z) * 2 * RING + t))
    return pairs


def add_powers(per, out, j, s):
    for k in range(per):
        for h in range(2):
            most = jnp.max(jnp.abs(out[s * per + k, j, h * WIDTH : (h + 1) * WIDTH, :]), axis=0, keepdims=True)
            power = jnp.ceil(jnp.log2(jnp.maximum(most, TINY)))
            out[s * per + k, j, 2 * WIDTH + 4 * h : 2 * WIDTH + 4 * h + 4, :] = jnp.broadcast_to(power, (4, QTOK))


def project_kernel(chunk, slots, acts, grads, proj, keep, give, av, gv, pv, sem_a, sem_g, sem_p):
    t = lax.axis_index("tensor")
    y, core = t // 2, t % 2
    per = chunk // QTOK
    d_in = acts.shape[2]
    weights, steps = [], []
    order = ((give, 2 * (1 - core), 0), (give, 2 * (1 - core), 1), (keep, 2 * core, 0), (keep, 2 * core, 1))
    for w, (out, first, j) in enumerate(order):
        layer = first + j
        weights.append(pltpu.make_async_copy(proj.at[layer], pv.at[w], sem_p.at[w]))
        for s in range(QUART // per):
            slot = len(steps) % slots
            group = []
            for k in range(per):
                rows = pl.ds(pl.multiple_of(flip(y, s * per + k) * QTOK, QTOK), QTOK)
                place = pl.ds(k * QTOK, QTOK)
                group.append(pltpu.make_async_copy(acts.at[layer, rows, :], av.at[slot, place, :], sem_a.at[slot, k]))
                group.append(pltpu.make_async_copy(grads.at[layer, rows, :], gv.at[slot, place, :], sem_g.at[slot, k]))
            steps.append((out, j, s, w, slot, group))
    for n in range(slots):
        if n == 0:
            weights[0].start()
        for c in steps[n][5]:
            c.start()
        if n == 0:
            for c in weights[1:]:
                c.start()
    for n, (out, j, s, w, slot, group) in enumerate(steps):
        if s == 0:
            weights[w].wait()
        for c in group:
            c.wait()
        parts = (
            lax.dot_general(pv[w, :, :d_in], av[slot], NT, preferred_element_type=jnp.float32),
            lax.dot_general(pv[w, :, d_in:], gv[slot], NT, preferred_element_type=jnp.float32),
        )
        if n > 0:
            add_powers(per, *steps[n - 1][:3])
        for h, part in enumerate(parts):
            for k in range(per):
                out[s * per + k, j, h * WIDTH : (h + 1) * WIDTH, :] = part[:, k * QTOK : (k + 1) * QTOK]
        if n + slots < len(steps):
            for c in steps[n + slots][5]:
                c.start()
    add_powers(per, *steps[-1][:3])


def project(acts, grads, proj, chunk, slots):
    layers, tokens, d_in, d_out = acts.shape[0], acts.shape[1], acts.shape[2], grads.shape[2]
    in_any = pl.BlockSpec(memory_space=pl.ANY)
    return pl.pallas_call(
        functools.partial(project_kernel, chunk, slots),
        in_specs=[in_any] * 3,
        out_specs=[pl.BlockSpec(memory_space=pltpu.VMEM)] * 2,
        out_shape=[jax.ShapeDtypeStruct((QUART, 2, ROWS, QTOK), jnp.float32)] * 2,
        scratch_shapes=[
            pltpu.VMEM((slots, chunk, d_in), jnp.bfloat16),
            pltpu.VMEM((slots, chunk, d_out), jnp.bfloat16),
            pltpu.VMEM((layers, WIDTH, d_in + d_out), jnp.bfloat16),
            pltpu.SemaphoreType.DMA((slots, chunk // QTOK)),
            pltpu.SemaphoreType.DMA((slots, chunk // QTOK)),
            pltpu.SemaphoreType.DMA((layers,)),
        ],
        compiler_params=pltpu.CompilerParams(vmem_limit_bytes=PROJECT_VMEM),
        cost_estimate=pl.CostEstimate(
            flops=2 * layers * tokens * (d_in + d_out) * WIDTH,
            bytes_accessed=2 * layers * tokens * (d_in + d_out),
            transcendentals=0,
        ),
        name="project",
    )(acts, grads, proj)


def score_tokens(scale, sums, q0, q1, q3, q2):
    core = lax.axis_index("tensor") % 2
    chip = lax.axis_index("dp")
    x, z = chip // RING, chip % RING

    def query(a, b, j):
        return (q0, q1, q2, q3)[a][b, j]

    acc = None
    for j in range(2):
        outs = sums[j, WIDTH : 2 * WIDTH, :]
        for a in range(RING):
            for b in range(RING):
                cx = jnp.where(core == 0, flip(x, b), flip(x, a))
                cz = jnp.where(core == 0, flip(z, a), flip(z, b))
                base = (cx * RING + cz) * 4
                feats = jnp.concatenate(
                    [(sums[j, pl.ds(base + i, 1), :] * outs).astype(jnp.bfloat16) for i in range(4)], 0
                )
                part = jnp.dot(query(a, b, j), feats, preferred_element_type=jnp.float32)
                acc = part if acc is None else acc + part
    return acc * scale


def own_score_kernel(scale, s0, q0, q1, q3, q2, out):
    out[...] = score_tokens(scale, s0, q0, q1, q3, q2)


def score_kernel(scale, own, s1, s2, s3, q0, q1, q3, q2, keep, give):
    y = lax.axis_index("tensor") // 2
    for d, sums in enumerate((None, s1, s2, s3)):
        acc = own[...] if d == 0 else score_tokens(scale, sums, q0, q1, q3, q2)
        place = pl.ds(pl.multiple_of(flip(y, d) * QTOK, QTOK), QTOK)
        keep[:, place] = acc[0:WIDTH]
        give[:, place] = acc[WIDTH : 2 * WIDTH]


def own_score(total, quers, scale):
    vm = pl.BlockSpec(memory_space=pltpu.VMEM)
    return pl.pallas_call(
        functools.partial(own_score_kernel, scale),
        in_specs=[vm] * 5,
        out_specs=vm,
        out_shape=jax.ShapeDtypeStruct((2 * WIDTH, QTOK), jnp.float32),
        compiler_params=pltpu.CompilerParams(vmem_limit_bytes=SCORE_VMEM),
        cost_estimate=pl.CostEstimate(flops=OWN_FLOPS, bytes_accessed=4 * 2**20, transcendentals=0),
        name="own_score",
    )(total, *quers)


def score(own, sums, quers, scale):
    vm = pl.BlockSpec(memory_space=pltpu.VMEM)
    shape = jax.ShapeDtypeStruct((WIDTH, QUART * QTOK), jnp.float32)
    return pl.pallas_call(
        functools.partial(score_kernel, scale),
        in_specs=[vm] * 8,
        out_specs=[vm] * 2,
        out_shape=[shape] * 2,
        compiler_params=pltpu.CompilerParams(vmem_limit_bytes=SCORE_VMEM),
        cost_estimate=pl.CostEstimate(
            flops=2 * 2 * 1024 * 4096 * 128, bytes_accessed=4 * 2**20, transcendentals=0
        ),
        name="score",
    )(own, *sums, *quers)


def after(value, other):
    return lax.optimization_barrier((value, other))[0]


def row_index():
    return lax.broadcasted_iota(jnp.int32, (1, ROWS, 1), 1)


def powers(message):
    row = row_index()
    first = message[:, 2 * WIDTH : 2 * WIDTH + 1].astype(jnp.float32)
    second = message[:, 2 * WIDTH + 4 : 2 * WIDTH + 5].astype(jnp.float32)
    return jnp.where((row < WIDTH) | ((row >= 2 * WIDTH) & (row < 2 * WIDTH + 4)), first, second)


def pack(values, power):
    scaled = values * jnp.exp2(TOP - power)
    return jnp.where(row_index() < 2 * WIDTH, scaled, power).astype(jnp.float16)


def unpack(message):
    return message.astype(jnp.float32) * jnp.exp2(powers(message) - TOP)


def local(activations, out_grads, proj_input, proj_output, query_feats):
    layers = activations.shape[0]
    width = proj_input.shape[1]
    scale = (layers * width * width) ** (-0.5)
    core = lax.axis_index("tensor") % 2
    both = ("dp", "tensor")

    theirs = lax.ppermute(query_feats, "tensor", swap_perm())
    mine = lax.dynamic_slice_in_dim(query_feats, 2 * core, 2, 0)
    got = lax.dynamic_slice_in_dim(theirs, 2 * core, 2, 0)
    proj = jnp.concatenate([proj_input, proj_output], axis=2)
    line0 = after(jnp.concatenate([mine, got], axis=1), proj)
    lines = [line0] + [lax.ppermute(line0, both, xz_perm(d, False)) for d in range(1, RING)]
    keep, give = project(activations, out_grads, proj, 512, 3)
    give, lines = lax.optimization_barrier((give, lines))
    plane0 = jnp.stack(lines)
    low = lax.ppermute(give[:2], "tensor", swap_perm())
    high = lax.ppermute(give[2:], "tensor", swap_perm())
    taken = [low[0], low[1], high[0], high[1]]
    part = [keep[d] + taken[d] for d in range(QUART)]
    power = [jnp.maximum(powers(keep[d]), powers(taken[d])) + 1.0 for d in range(QUART)]
    packed = [pack(part[d], power[d]) for d in range(1, QUART)]
    sent = [None] * 3
    for d in ORDER:
        sent[d - 1] = lax.ppermute(packed[d - 1], "tensor", y_perm(d))
    plane1 = lax.ppermute(plane0, both, xz_perm(1, True))
    total = part[0] + sum(unpack(m) for m in sent)
    top = power[0]
    for m in sent:
        top = jnp.maximum(top, powers(m))
    message = pack(total, top + 2.0)
    late = [lax.ppermute(p, both, xz_perm(3, True)) for p in (after(plane0, packed[2]), after(plane1, sent[1]))]
    quers = [plane0, plane1, *late]
    own = own_score(total[:, : 2 * WIDTH], quers, scale)
    sums = [None] * 3
    for d in ORDER:
        sums[d - 1] = unpack(after(lax.ppermute(message, "tensor", y_perm(d)), own))[:, : 2 * WIDTH]

    keep_s, give_s = score(own, sums, quers, scale)
    return (keep_s + lax.ppermute(give_s, "tensor", swap_perm())).T


def solution(mesh):
    in_specs = (
        P(None, "dp", "tensor"),
        P(None, "dp", "tensor"),
        P(None, None, "tensor"),
        P(None, None, "tensor"),
        P(None, "tensor", "dp"),
    )
    out_specs = P("dp", "tensor")
    return jax.shard_map(local, mesh=mesh, in_specs=in_specs, out_specs=out_specs, check_vma=False)
```
